32 devices in a mesh: dp: 4 (over y, core), fsdp: 8 (over z, x).
Axes of the slice: x: 2, y: 2, z: 4, core: 2. Of those that a mesh axis runs over, the one named last changes fastest.
Arguments:
- activations: bfloat16 [4096, 8192], P(('dp', 'fsdp')), may hold values from -630 to 630, as said below
- gain: bfloat16 [8192], P('fsdp'), may hold values from 0.25 to 1.75
- key_weight: bfloat16 [8192, 512], P('fsdp'), may hold values from -0.0625 to 0.0625
- key_gain: float32 [128], replicated, may hold values from 0.25 to 1.75
- cotangent: bfloat16 [4096, 512], P(('dp', 'fsdp')), may hold values from -6 to 6
- directions: bfloat16 [8192, 8], P('fsdp'), may hold values from -6 to 6
Outputs:
- ortho_basis: float32 [8192, 8], P('fsdp')
- grad: float32 [8192], P('fsdp')
The draws below stay inside these ranges and needn't reach their ends.
Inputs may be any that keep to these rules, and one draw needn't show every extreme that they name: The block's input activations.
All inputs are finite; a program needn't handle non-finite values.
Results may differ from the reference program's by a relative error of at most 0.01.
Values may be sent and summed in bfloat16 or wider, within the bound.
A program may use at most 128 MiB of HBM per device.

```python
import math
import jax
import jax.numpy as jnp
from jax import lax

D = 8192
HEADS_KV = 4
HEAD_DIM = 128
DIRS = 8
TOKENS = 4096


def draw_activations(key, part):
    first, second, third = jax.random.split(key, 3)
    row_scale = jnp.exp(jax.random.uniform(second, (TOKENS, 1), minval=0.0, maxval=math.log(10.0)))
    ramp = jnp.exp(math.log(3.0) * jnp.arange(D, dtype=jnp.float32)[None, :] / (D - 1))
    jitter = jnp.exp(jax.random.uniform(third, (1, D), minval=0.0, maxval=math.log(3.5)))
    base = jnp.clip(jax.random.normal(first, (TOKENS, D)), -6.0, 6.0)
    return (base * row_scale * ramp * jitter).astype(jnp.bfloat16)


def block_levels(own_key, shape, cuts, low, high):
    level = 1.0
    for dim, parts in cuts:
        heights = jax.random.uniform(jax.random.fold_in(jax.random.fold_in(own_key, 6), dim), (parts,), jnp.float32, low / len(cuts), high / len(cuts))
        level = level * jnp.repeat(jnp.exp(heights), shape[dim] // parts).reshape((-1,) + (1,) * (len(shape) - 1 - dim))
    return level


def normal_values(own_key, extent, scale, reach, cuts=(), kind=jnp.bfloat16):
    values = jax.random.normal(own_key, extent, jnp.float32) * scale
    if len(cuts) > 0:
        values = block_levels(own_key, extent, cuts, -0.22, 0.18) * values
    return jnp.clip(values, min=-reach, max=reach).astype(kind)


def setup_inputs(seed: int = 0) -> dict:
    splits = jax.random.split(jax.random.key(seed), 7)
    return {
        "activations": draw_activations(jax.random.fold_in(splits[6], 71), 0),
        "gain": jnp.clip(1.0 + 0.15 * jax.random.normal(splits[1], (D,), jnp.float32), 0.25, 1.75).astype(jnp.bfloat16),
        "key_weight": normal_values(splits[2], (D, HEADS_KV * HEAD_DIM), D ** -0.5, 0.0625, ((0, 8),)),
        "key_gain": jnp.clip(1.0 + 0.15 * jax.random.normal(splits[3], (HEAD_DIM,), jnp.float32), 0.25, 1.75),
        "cotangent": normal_values(splits[4], (TOKENS, HEADS_KV * HEAD_DIM), 1.0, 6.0, ((0, 32),)),
        "directions": normal_values(splits[5], (D, DIRS), 1.0, 6.0, ((0, 8),)),
    }


def key_stats(key_rows, weighted_flat):
    shaped = key_rows.reshape(key_rows.shape[0], HEADS_KV, HEAD_DIM)
    key_scale = jnp.sqrt(lax.optimization_barrier(jnp.mean(shaped * shaped, axis=-1, keepdims=True)) + 1e-05)
    unit_keys = shaped / key_scale
    weighted = weighted_flat.reshape(shaped.shape)
    inner_sum = lax.optimization_barrier(jnp.sum(unit_keys * weighted, axis=-1, keepdims=True))
    grad_keys = (weighted - unit_keys * inner_sum / HEAD_DIM) / key_scale
    return (key_scale, unit_keys, weighted, inner_sum, grad_keys)

def second_order(tangent_keys, key_scale, unit_keys, weighted, inner_sum, grad_keys):
    shift_rate = lax.optimization_barrier(jnp.sum(unit_keys * tangent_keys, axis=-1, keepdims=True)) / HEAD_DIM
    unit_change = (tangent_keys - unit_keys * shift_rate) / key_scale
    along = lax.optimization_barrier(jnp.sum(unit_change * weighted, axis=-1, keepdims=True))
    return -(unit_change * inner_sum + unit_keys * along) / (HEAD_DIM * key_scale) - grad_keys * shift_rate / key_scale

def block_terms(input_rows, cot_rows, gain, key_weight, key_gain, directions):
    values = input_rows.astype(jnp.float32)
    normed = values / jnp.sqrt(lax.optimization_barrier(jnp.mean(values * values, axis=1, keepdims=True)) + 1e-05)
    scaled_in = (normed * gain.astype(jnp.float32)[None, :]).astype(jnp.bfloat16)
    key_rows = jnp.dot(scaled_in.astype(jnp.float32), key_weight.astype(jnp.float32), preferred_element_type=jnp.float32)
    weighted_flat = cot_rows.astype(jnp.float32) * jnp.tile(key_gain, HEADS_KV)[None, :]
    key_scale, unit_keys, weighted, inner_sum, grad_keys = key_stats(key_rows, weighted_flat)
    row_count = input_rows.shape[0]
    lifted = (normed[None] * directions.astype(jnp.float32).T[:, None, :]).astype(jnp.bfloat16)
    tangent_keys = jnp.dot(lifted.reshape(-1, D).astype(jnp.float32), key_weight.astype(jnp.float32), preferred_element_type=jnp.float32)
    tangent_keys = tangent_keys.reshape(DIRS, row_count, HEADS_KV, HEAD_DIM)
    second = second_order(tangent_keys, key_scale, unit_keys, weighted, inner_sum, grad_keys)
    back_rows = jnp.concatenate([grad_keys[None], second], axis=0).astype(jnp.bfloat16)
    back_rows = back_rows.reshape(-1, HEADS_KV * HEAD_DIM)
    spread = jnp.dot(back_rows.astype(jnp.float32), key_weight.T.astype(jnp.float32), preferred_element_type=jnp.float32)
    spread = spread.reshape(DIRS + 1, row_count, D)
    return lax.optimization_barrier(jnp.sum(spread * normed[None], axis=1))

def reference(activations, gain, key_weight, key_gain, cotangent, directions):
    token_block = math.gcd(TOKENS, 1024)
    block_count = TOKENS // token_block

    def add_block(running, position):
        begin_row = (position * token_block).astype(jnp.int32)
        input_rows = lax.dynamic_slice_in_dim(activations, begin_row, token_block, 0)
        cot_rows = lax.dynamic_slice_in_dim(cotangent, begin_row, token_block, 0)
        return (running + block_terms(input_rows, cot_rows, gain, key_weight, key_gain, directions), None)
    running, _ = lax.scan(add_block, jnp.zeros((DIRS + 1, D), jnp.float32), jnp.arange(block_count, dtype=jnp.int32))
    terms = running / math.sqrt(TOKENS)
    grad = terms[0]
    images = terms[1:]
    gram_matrix = jnp.dot(images, images.T, precision=lax.Precision.HIGHEST)
    factor = jnp.linalg.cholesky(gram_matrix)
    ortho_basis = math.sqrt(D) * jax.scipy.linalg.solve_triangular(factor, images, lower=True)
    return (ortho_basis.T, grad)
```

```python
import functools
import math

import jax
import jax.numpy as jnp
from jax import lax
from jax.experimental import pallas as pl
from jax.experimental.pallas import tpu as pltpu
from jax.sharding import PartitionSpec as P

D = 8192
HEADS_KV = 4
HEAD_DIM = 128
PAD = 16
MESH = pl.DeviceIdType.MESH
Z, Y1, DZ, DY1, X, Y2, DX, DY2 = range(8)
ZB = 8
F32 = jnp.float32


def kernel(
    n, n_dp, groups, total_tokens,
    act_ref, w_ref, dg_ref, key_gain_ref, cot_ref,
    ortho_ref, grad_ref,
    wbuf, lifted, acc, back, part, rbuf, xbuf, gbuf, rstd,
    send_sem, recv_sem, part_send, part_recv, dp_send, dp_recv, gram_send, gram_recv,
):
    line = n // 2
    steps = line * groups
    tokens = act_ref.shape[0]
    rows = w_ref.shape[0]
    rows_g = rows // (2 * groups)
    unit = rows_g // 4
    count = back.shape[0] // tokens
    dp, me = lax.axis_index("dp"), lax.axis_index("fsdp")
    core, y = lax.rem(dp, 2), dp // 2
    z, x = me // 2, lax.rem(me, 2)
    sibling = dp + 1 - 2 * core
    y_peer = lax.rem(dp + 2, n_dp)
    x_peer = me + 1 - 2 * x

    barrier = pltpu.get_barrier_semaphore()

    def greet_fsdp(b, _):
        pl.semaphore_signal(
            barrier, inc=1, device_id=(dp, lax.rem(me + 1 + b, n)), device_id_type=MESH
        )
        return 0

    def greet_dp(b, _):
        pl.semaphore_signal(
            barrier, inc=1, device_id=(lax.rem(dp + 1 + b, n_dp), me), device_id_type=MESH
        )
        return 0

    lax.fori_loop(0, n - 1, greet_fsdp, 0)
    lax.fori_loop(0, n_dp - 1, greet_dp, 0)

    def place(zp, xp, cp, g):
        return ((zp * 2 + xp) * 2 + cp) * groups + g

    for cg in range(2 * groups):
        at = me * 2 * groups + cg
        wbuf[at, 0 : 2 * unit] = w_ref[cg * rows_g : cg * rows_g + 2 * unit]
        wbuf[at, 2 * unit : 2 * unit + PAD] = dg_ref[cg]
        wbuf[at, 2 * unit + PAD :] = w_ref[cg * rows_g + 2 * unit : (cg + 1) * rows_g]

    room = jnp.minimum(z, line - 1 - z)
    wide = jnp.where(z < line - 1 - z, 1, -1)

    def source(k):
        near = k <= 2 * room
        dist = jnp.where(near, (k + 1) // 2, k - room)
        sign = jnp.where(near, jnp.where(lax.rem(k, 2) == 1, -1, 1), wide)
        return z + sign * dist, sign

    def span(kind, first, sent):
        side = y if sent else 1 - y
        if kind in (Z, ZB, DZ) or (first and kind in (X, DX)):
            start, size = y * unit, 3 * unit + PAD
        elif kind in (X, DX):
            start, size = y * (2 * unit), 2 * unit + PAD
        else:
            if kind in (DY1, DY2):
                side = 1 - y if sent else y
                side = 1 - y
            if kind in (Y1, DY1) or first:
                start, size = side * (3 * unit + PAD), unit
            else:
                start, size = side * (2 * unit + PAD), 2 * unit
        return pl.ds(pl.multiple_of(start, 16), size)

    def copy(kind, i, first, sent):
        k, g = i // groups, lax.rem(i, groups)
        zp, sign = source(k)
        own_column = kind in (Z, ZB, Y1, DZ, DY1)
        to_sibling = kind in (DZ, DY1, DX, DY2)
        if kind == X and sent:
            own_column = True
        column = x if own_column else 1 - x
        half = (core if sent else 1 - core) if to_sibling else core
        if kind == ZB:
            device = (dp, me - 2)
        elif kind == Z:
            device = (dp, me + 2) if first else (dp, me - 2 * sign)
        elif kind == X:
            device = (dp, x_peer)
        elif kind in (Y1, Y2):
            device = (y_peer, me)
        else:
            device = (sibling, me)
        ref = wbuf.at[place(zp, column, half, g), span(kind, first, sent)]
        arrival = Z if kind == ZB else kind
        return pltpu.make_async_remote_copy(
            src_ref=ref,
            dst_ref=ref,
            send_sem=send_sem.at[kind, i],
            recv_sem=recv_sem.at[arrival, zp * groups + g],
            device_id=device,
            device_id_type=MESH,
        )

    def start(kind, i, first=False):
        copy(kind, i, first, True).start()

    def arrive(kind, i, first=False):
        copy(kind, i, first, False).wait_recv()

    def sent(kind, i, first=False):
        copy(kind, i, first, True).wait_send()

    def passes_on(i):
        sign = source(i // groups)[1]
        onward = z - sign
        return (onward >= 0) & (onward < line)

    def square_sum(q, run):
        part_in = act_ref[:, pl.ds(pl.multiple_of(q * 512, 512), 512)].astype(F32)
        return run + jnp.sum(part_in * part_in, axis=1, keepdims=True)

    width = act_ref.shape[1]
    square = lax.fori_loop(0, width // 512, square_sum, jnp.zeros((tokens, 1), F32))
    rstd[...] = jnp.broadcast_to(1.0 / jnp.sqrt(square / width + 1e-05), rstd.shape)
    acc[...] = jnp.zeros_like(acc)

    pl.semaphore_wait(barrier, n - 1 + n_dp - 1)

    for g in range(groups):

        @pl.when(z + 1 < line)
        def _():
            start(Z, g, True)

        @pl.when(z >= 1)
        def _():
            start(ZB, g, True)

        start(X, g, True)

    def normed_at(feature, size):
        values = act_ref[:, pl.ds(pl.multiple_of(feature, 128), size)].astype(F32)
        return values * rstd[:, 0:1]

    def weight_at(at):
        return jnp.concatenate(
            [wbuf[at, 0 : 2 * unit], wbuf[at, 2 * unit + PAD : 4 * unit + PAD]], axis=0
        )

    def forward(zp, xp, g):
        for cp in range(2):
            at = place(zp, xp, cp, g)
            normed = normed_at((zp * 2 + xp) * rows + (cp * groups + g) * rows_g, rows_g)
            factors = wbuf[at, 2 * unit : 2 * unit + PAD, 0:rows_g].astype(F32)
            for j in range(count):
                lifted[j * tokens : (j + 1) * tokens, cp * rows_g : (cp + 1) * rows_g] = (
                    normed * factors[j : j + 1]
                ).astype(jnp.bfloat16)
        weight = jnp.concatenate(
            [weight_at(place(zp, xp, 0, g)), weight_at(place(zp, xp, 1, g))], axis=0
        )
        for h in range(2):
            half = slice(h * 256, (h + 1) * 256)
            acc[:, half] += jnp.dot(
                lifted[...], weight[:, half], preferred_element_type=F32
            )

    def forward_own(g, _):
        forward(z, x, g)
        return 0

    lax.fori_loop(0, groups, forward_own, 0)

    def cross_arrived(i, first):
        arrive(X, i, first)
        start(Y2, i, first)
        start(DX, i, first)

    def turn(t, _):
        i = t + groups

        @pl.when(i < steps)
        def _():
            arrive(Z, i)

            @pl.when(passes_on(i))
            def _():
                start(Z, i)

            start(X, i)
            start(Y1, i)
            start(DZ, i)

        if groups > 1:

            @pl.when(t == 0)
            def _():
                for early in range(groups - 1):
                    cross_arrived(early, True)

        i1 = t + groups - 1

        @pl.when(i1 < groups)
        def _():
            cross_arrived(i1, True)

        @pl.when((i1 >= groups) & (i1 < steps))
        def _():
            cross_arrived(i1, False)
            arrive(Y1, i1)
            start(DY1, i1)

        i2 = t + groups - 2

        @pl.when((i2 >= 0) & (i2 < groups))
        def _():
            arrive(Y2, i2, True)
            start(DY2, i2, True)

        @pl.when((i2 >= groups) & (i2 < steps))
        def _():
            arrive(Y2, i2)
            start(DY2, i2)
            arrive(DZ, i2)
            arrive(DY1, i2)
            forward(source(i2 // groups)[0], x, lax.rem(i2, groups))

        i3 = t + groups - 3

        @pl.when((i3 >= 0) & (i3 < groups))
        def _():
            arrive(DX, i3, True)
            arrive(DY2, i3, True)

        @pl.when((i3 >= groups) & (i3 < steps))
        def _():
            arrive(DX, i3)
            arrive(DY2, i3)

        @pl.when((i3 >= 0) & (i3 < steps))
        def _():
            forward(source(i3 // groups)[0], 1 - x, lax.rem(i3, groups))

        return 0

    lax.fori_loop(0, steps + 3 - groups, turn, 0)

    for h in range(HEADS_KV):
        cols = slice(h * HEAD_DIM, (h + 1) * HEAD_DIM)
        key = acc[0:tokens, cols]
        inv_scale = 1.0 / jnp.sqrt(
            jnp.sum(key * key, axis=1, keepdims=True) / HEAD_DIM + 1e-05
        )
        unit_key = key * inv_scale
        weighted = cot_ref[:, cols].astype(F32) * key_gain_ref[...]
        inner = jnp.sum(unit_key * weighted, axis=1, keepdims=True)
        back[0:tokens, cols] = (
            (weighted - unit_key * (inner / HEAD_DIM)) * inv_scale
        ).astype(jnp.bfloat16)
        inv_square = inv_scale * inv_scale

        def one_direction(j, _):
            at = pl.ds(pl.multiple_of(j * tokens, 128), tokens)
            tangent = acc[at, cols]
            shift = jnp.sum(unit_key * tangent, axis=1, keepdims=True) / HEAD_DIM
            across = jnp.sum(weighted * tangent, axis=1, keepdims=True)
            by_tangent = -inner * inv_square / HEAD_DIM
            by_key = (3.0 * shift * inner - across) * inv_square / HEAD_DIM
            by_weight = -shift * inv_square
            back[at, cols] = (
                tangent * by_tangent + unit_key * by_key + weighted * by_weight
            ).astype(jnp.bfloat16)
            return 0

        lax.fori_loop(1, count, one_direction, 0)

    def terms_of(owner):
        def one_group(cg, _):
            weight = weight_at(owner * 2 * groups + cg)
            normed = normed_at(owner * rows + cg * rows_g, rows_g)
            product = lax.dot_general(
                back[...], weight, (((1,), (1,)), ((), ())), preferred_element_type=F32
            )
            cols = pl.ds(pl.multiple_of(cg * rows_g, 128), rows_g)
            for j in range(count):
                part[owner, j : j + 1, cols] = jnp.sum(
                    product[j * tokens : (j + 1) * tokens] * normed, axis=0, keepdims=True
                )
            return 0

        lax.fori_loop(0, 2 * groups, one_group, 0)

    def part_copy(b):
        owner = lax.rem(me + 1 + b, n)
        return pltpu.make_async_remote_copy(
            src_ref=part.at[owner],
            dst_ref=rbuf.at[me],
            send_sem=part_send.at[owner],
            recv_sem=part_recv.at[me],
            device_id=(dp, owner),
            device_id_type=MESH,
        )

    def send_part(b, _):
        terms_of(lax.rem(me + 1 + b, n))
        part_copy(b).start()
        return 0

    lax.fori_loop(0, n - 1, send_part, 0)
    terms_of(me)

    def take_part(b, run):
        other = lax.rem(me + n - 1 - b, n)
        pltpu.make_async_remote_copy(
            src_ref=part.at[other],
            dst_ref=rbuf.at[other],
            send_sem=part_send.at[other],
            recv_sem=part_recv.at[other],
            device_id=(dp, other),
            device_id_type=MESH,
        ).wait_recv()
        return run + rbuf[other]

    xbuf[dp] = lax.fori_loop(0, n - 1, take_part, part[me])

    def dp_copy(b, slot):
        other = lax.rem(dp + 1 + b, n_dp)
        return pltpu.make_async_remote_copy(
            src_ref=xbuf.at[dp if slot else other],
            dst_ref=xbuf.at[dp if slot else other],
            send_sem=dp_send.at[b],
            recv_sem=dp_recv.at[dp if slot else other],
            device_id=(other, me),
            device_id_type=MESH,
        )

    for b in range(n_dp - 1):
        dp_copy(b, True).start()
    for b in range(n_dp - 1):
        dp_copy(b, False).wait_recv()
    summed = xbuf[0]
    for d in range(1, n_dp):
        summed = summed + xbuf[d]
    summed = summed / math.sqrt(total_tokens)
    grad_ref[...] = summed[0:1]
    images = summed[1:count]
    dirs = count - 1
    lane = lax.broadcasted_iota(jnp.int32, (dirs, 128), 1)
    gram = jnp.zeros((dirs, 128), F32)
    for j in range(dirs):
        gram = jnp.where(
            lane == j, jnp.sum(images * images[j : j + 1], axis=1, keepdims=True), gram
        )
    gbuf[me] = gram

    def gram_copy(b, slot):
        other = lax.rem(me + 1 + b, n)
        return pltpu.make_async_remote_copy(
            src_ref=gbuf.at[me if slot else other],
            dst_ref=gbuf.at[me if slot else other],
            send_sem=gram_send.at[b],
            recv_sem=gram_recv.at[me if slot else other],
            device_id=(dp, other),
            device_id_type=MESH,
        )

    def start_gram(b, _):
        gram_copy(b, True).start()
        return 0

    def take_gram(b, _):
        gram_copy(b, False).wait_recv()
        return 0

    lax.fori_loop(0, n - 1, start_gram, 0)
    lax.fori_loop(0, n - 1, take_gram, 0)
    gram = lax.fori_loop(1, n, lambda s, run: run + gbuf[s], gbuf[0])

    row = lax.broadcasted_iota(jnp.int32, (dirs, 1), 0)
    for j in range(dirs):
        inverse = 1.0 / jnp.sqrt(gram[j : j + 1, j : j + 1])
        gram_row = gram[j : j + 1] * inverse
        image_row = images[j : j + 1] * inverse
        factor = jnp.where(row > j, gram[:, j : j + 1] * inverse, 0.0)
        gram = jnp.where(row == j, gram_row, gram - factor * gram_row)
        images = jnp.where(row == j, image_row, images - factor * image_row)
    ortho_ref[...] = math.sqrt(D) * images

    for g in range(groups):

        @pl.when(z + 1 < line)
        def _():
            sent(Z, g, True)

        @pl.when(z >= 1)
        def _():
            sent(ZB, g, True)

        for kind in (X, Y2, DX, DY2):
            sent(kind, g, True)

    def drain(i, _):
        @pl.when(passes_on(i))
        def _():
            sent(Z, i)

        for kind in (X, Y1, DZ, DY1, Y2, DX, DY2):
            sent(kind, i)
        return 0

    lax.fori_loop(groups, steps, drain, 0)

    def drain_parts(b, _):
        part_copy(b).wait_send()
        gram_copy(b, True).wait_send()
        return 0

    lax.fori_loop(0, n - 1, drain_parts, 0)
    for b in range(n_dp - 1):
        dp_copy(b, True).wait_send()


def per_device(n, n_dp, activations, gain, key_weight, key_gain, cotangent, directions):
    tokens, width = activations.shape
    rows, width_keys = key_weight.shape
    count = directions.shape[1] + 1
    groups = 2 if rows >= 1024 else 1
    rows_g = rows // (2 * groups)
    steps = n // 2 * groups
    factors = jnp.concatenate(
        [gain[None], directions.T, jnp.zeros((PAD - count, rows), jnp.bfloat16)], axis=0
    )
    factors = factors.reshape(PAD, 2 * groups, rows_g).transpose(1, 0, 2)
    factors = jnp.pad(factors, ((0, 0), (0, 0), (0, width_keys - rows_g)))
    vmem = pl.BlockSpec(memory_space=pltpu.VMEM)
    dma = pltpu.SemaphoreType.DMA
    flops = 4 * count * tokens * width * width_keys
    ortho, grad = pl.pallas_call(
        functools.partial(kernel, n, n_dp, groups, tokens * n * n_dp),
        out_shape=(
            jax.ShapeDtypeStruct((count - 1, rows), F32),
            jax.ShapeDtypeStruct((1, rows), F32),
        ),
        in_specs=[vmem] * 5,
        out_specs=(vmem, vmem),
        scratch_shapes=[
            pltpu.VMEM((n * 2 * groups, rows_g + PAD, width_keys), jnp.bfloat16),
            pltpu.VMEM((count * tokens, 2 * rows_g), jnp.bfloat16),
            pltpu.VMEM((count * tokens, width_keys), F32),
            pltpu.VMEM((count * tokens, width_keys), jnp.bfloat16),
            pltpu.VMEM((n, count, rows), F32),
            pltpu.VMEM((n, count, rows), F32),
            pltpu.VMEM((n_dp, count, rows), F32),
            pltpu.VMEM((n, count - 1, 128), F32),
            pltpu.VMEM((tokens, 128), F32),
            dma((9, steps)),
            dma((8, steps)),
            dma((n,)),
            dma((n,)),
            dma((n_dp,)),
            dma((n_dp,)),
            dma((n,)),
            dma((n,)),
        ],
        compiler_params=pltpu.CompilerParams(
            collective_id=0, has_side_effects=True, vmem_limit_bytes=48 * 1024 * 1024
        ),
        cost_estimate=pl.CostEstimate(flops=flops, bytes_accessed=4 * 2**20, transcendentals=0),
    )(activations, key_weight, factors, key_gain[None], cotangent)
    return (ortho.T, grad[0])


def solution(mesh):
    placed = (
        P(("dp", "fsdp"), None),
        P("fsdp"),
        P("fsdp", None),
        P(),
        P(("dp", "fsdp"), None),
        P("fsdp", None),
    )
    return jax.shard_map(
        functools.partial(per_device, mesh.shape["fsdp"], mesh.shape["dp"]),
        mesh=mesh,
        in_specs=placed,
        out_specs=(P("fsdp", None), P("fsdp")),
        check_vma=False,
    )
```

```python
import functools
import math

import jax
import jax.numpy as jnp
from jax import lax
from jax.experimental import pallas as pl
from jax.experimental.pallas import tpu as pltpu
from jax.sharding import PartitionSpec as P

D = 8192
HEADS_KV = 4
HEAD_DIM = 128
PAD = 16
MESH = pl.DeviceIdType.MESH
Z, Y1, DZ, DY1, X, Y2, DX, DY2 = range(8)
ZB = 8
F32 = jnp.float32


def kernel(
    n, n_dp, groups, total_tokens,
    act_in, w_ref, dg_ref, key_gain_ref, cot_in,
    ortho_ref, grad_ref,
    act_ref, cot_ref, wbuf, lifted, acc, back, part, rbuf, xbuf, gbuf, nbuf, own_sem, in_sem,
    send_sem, recv_sem, part_send, part_recv, dp_send, dp_recv, gram_send, gram_recv,
):
    line = n // 2
    steps = line * groups
    tokens = act_ref.shape[0]
    rows = w_ref.shape[0]
    rows_g = rows // (2 * groups)
    unit = rows_g // 4
    count = back.shape[0] // tokens
    dp, me = lax.axis_index("dp"), lax.axis_index("fsdp")
    core, y = lax.rem(dp, 2), dp // 2
    z, x = me // 2, lax.rem(me, 2)
    sibling = dp + 1 - 2 * core
    y_peer = lax.rem(dp + 2, n_dp)
    x_peer = me + 1 - 2 * x

    barrier = pltpu.get_barrier_semaphore()

    def greet_fsdp(b, _):
        pl.semaphore_signal(
            barrier, inc=1, device_id=(dp, lax.rem(me + 1 + b, n)), device_id_type=MESH
        )
        return 0

    def greet_dp(b, _):
        pl.semaphore_signal(
            barrier, inc=1, device_id=(lax.rem(dp + 1 + b, n_dp), me), device_id_type=MESH
        )
        return 0

    lax.fori_loop(0, n - 1, greet_fsdp, 0)
    lax.fori_loop(0, n_dp - 1, greet_dp, 0)

    def place(zp, xp, cp, g):
        return ((zp * 2 + xp) * 2 + cp) * groups + g

    own_copies = []
    for cg in range(2 * groups):
        at = me * 2 * groups + cg
        top, low = cg * rows_g, cg * rows_g + 2 * unit
        own_copies += [
            pltpu.make_async_copy(
                w_ref.at[top : top + 2 * unit], wbuf.at[at, 0 : 2 * unit], own_sem.at[0, cg]
            ),
            pltpu.make_async_copy(
                w_ref.at[low : low + 2 * unit],
                wbuf.at[at, 2 * unit + PAD : 4 * unit + PAD],
                own_sem.at[1, cg],
            ),
            pltpu.make_async_copy(
                dg_ref.at[cg], wbuf.at[at, 2 * unit : 2 * unit + PAD], own_sem.at[2, cg]
            ),
        ]
    for one in own_copies:
        one.start()
    act_copy = pltpu.make_async_copy(act_in, act_ref, in_sem.at[0])
    cot_copy = pltpu.make_async_copy(cot_in, cot_ref, in_sem.at[1])
    act_copy.start()
    cot_copy.start()

    room = jnp.minimum(z, line - 1 - z)
    wide = jnp.where(z < line - 1 - z, 1, -1)

    def source(k):
        near = k <= 2 * room
        dist = jnp.where(near, (k + 1) // 2, k - room)
        sign = jnp.where(near, jnp.where(lax.rem(k, 2) == 1, -1, 1), wide)
        return z + sign * dist, sign

    def span(kind, first, sent):
        side = y if sent else 1 - y
        if kind in (Z, ZB, DZ) or (first and kind in (X, DX)):
            start, size = y * unit, 3 * unit + PAD
        elif kind in (X, DX):
            start, size = y * (2 * unit), 2 * unit + PAD
        else:
            if kind in (DY1, DY2):
                side = 1 - y if sent else y
                side = 1 - y
            if kind in (Y1, DY1) or first:
                start, size = side * (3 * unit + PAD), unit
            else:
                start, size = side * (2 * unit + PAD), 2 * unit
        return pl.ds(pl.multiple_of(start, 16), size)

    def copy(kind, i, first, sent):
        k, g = i // groups, lax.rem(i, groups)
        zp, sign = source(k)
        own_column = kind in (Z, ZB, Y1, DZ, DY1)
        to_sibling = kind in (DZ, DY1, DX, DY2)
        if kind == X and sent:
            own_column = True
        column = x if own_column else 1 - x
        half = (core if sent else 1 - core) if to_sibling else core
        if kind == ZB:
            device = (dp, me - 2)
        elif kind == Z:
            device = (dp, me + 2) if first else (dp, me - 2 * sign)
        elif kind == X:
            device = (dp, x_peer)
        elif kind in (Y1, Y2):
            device = (y_peer, me)
        else:
            device = (sibling, me)
        ref = wbuf.at[place(zp, column, half, g), span(kind, first, sent)]
        arrival = Z if kind == ZB else kind
        return pltpu.make_async_remote_copy(
            src_ref=ref,
            dst_ref=ref,
            send_sem=send_sem.at[kind, i],
            recv_sem=recv_sem.at[arrival, zp * groups + g],
            device_id=device,
            device_id_type=MESH,
        )

    def start(kind, i, first=False):
        copy(kind, i, first, True).start()

    def arrive(kind, i, first=False):
        copy(kind, i, first, False).wait_recv()

    def sent(kind, i, first=False):
        copy(kind, i, first, True).wait_send()

    def passes_on(i):
        sign = source(i // groups)[1]
        onward = z - sign
        return (onward >= 0) & (onward < line)

    pl.semaphore_wait(barrier, n - 1 + n_dp - 1)
    for one in own_copies:
        one.wait()

    for g in range(groups):

        @pl.when(z + 1 < line)
        def _():
            start(Z, g, True)

        @pl.when(z >= 1)
        def _():
            start(ZB, g, True)

        start(X, g, True)

    acc[...] = jnp.zeros_like(acc)
    act_copy.wait()

    width = act_ref.shape[1]

    def square_sum(q, run):
        part_in = act_ref[:, pl.ds(pl.multiple_of(q * 512, 512), 512)].astype(F32)
        part_in = part_in * part_in
        for h in range(4):
            run = run + part_in[:, h * 128 : (h + 1) * 128]
        return run

    square = lax.fori_loop(0, width // 512, square_sum, jnp.zeros((tokens, 128), F32))
    square = jnp.sum(square, axis=1, keepdims=True)
    rstd = jnp.broadcast_to(1.0 / jnp.sqrt(square / width + 1e-05), (tokens, 512))

    def normalize(q, _):
        cols = pl.ds(pl.multiple_of(q * 512, 512), 512)
        nbuf[:, cols] = act_ref[:, cols].astype(F32) * rstd
        return 0

    lax.fori_loop(0, width // 512, normalize, 0)

    def normed_at(feature, size):
        return nbuf[:, pl.ds(pl.multiple_of(feature, 128), size)]

    def weight_at(at):
        return jnp.concatenate(
            [wbuf[at, 0 : 2 * unit], wbuf[at, 2 * unit + PAD : 4 * unit + PAD]], axis=0
        )

    def forward(zp, xp, g):
        for cp in range(2):
            at = place(zp, xp, cp, g)
            normed = normed_at((zp * 2 + xp) * rows + (cp * groups + g) * rows_g, rows_g)
            factors = wbuf[at, 2 * unit : 2 * unit + PAD, 0:rows_g].astype(F32)
            for j in range(count):
                lifted[j * tokens : (j + 1) * tokens, cp * rows_g : (cp + 1) * rows_g] = (
                    normed * factors[j : j + 1]
                ).astype(jnp.bfloat16)
        weight = jnp.concatenate(
            [weight_at(place(zp, xp, 0, g)), weight_at(place(zp, xp, 1, g))], axis=0
        )
        for h in range(2):
            half = slice(h * 256, (h + 1) * 256)
            acc[:, half] += jnp.dot(
                lifted[...], weight[:, half], preferred_element_type=F32
            )

    def forward_own(g, _):
        forward(z, x, g)
        return 0

    lax.fori_loop(0, groups, forward_own, 0)

    def cross_arrived(i, first):
        arrive(X, i, first)
        start(Y2, i, first)
        start(DX, i, first)

    def turn(t, _):
        i = t + groups

        @pl.when(i < steps)
        def _():
            arrive(Z, i)

            @pl.when(passes_on(i))
            def _():
                start(Z, i)

            start(X, i)
            start(Y1, i)
            start(DZ, i)

        if groups > 1:

            @pl.when(t == 0)
            def _():
                for early in range(groups - 1):
                    cross_arrived(early, True)

        i1 = t + groups - 1

        @pl.when(i1 < groups)
        def _():
            cross_arrived(i1, True)

        @pl.when((i1 >= groups) & (i1 < steps))
        def _():
            cross_arrived(i1, False)
            arrive(Y1, i1)
            start(DY1, i1)

        i2 = t + groups - 2

        @pl.when((i2 >= 0) & (i2 < groups))
        def _():
            arrive(Y2, i2, True)
            start(DY2, i2, True)

        @pl.when((i2 >= groups) & (i2 < steps))
        def _():
            arrive(Y2, i2)
            start(DY2, i2)
            arrive(DZ, i2)
            arrive(DY1, i2)
            forward(source(i2 // groups)[0], x, lax.rem(i2, groups))

        i3 = t + groups - 3

        @pl.when((i3 >= 0) & (i3 < groups))
        def _():
            arrive(DX, i3, True)
            arrive(DY2, i3, True)

        @pl.when((i3 >= groups) & (i3 < steps))
        def _():
            arrive(DX, i3)
            arrive(DY2, i3)

        @pl.when((i3 >= 0) & (i3 < steps))
        def _():
            forward(source(i3 // groups)[0], 1 - x, lax.rem(i3, groups))

        return 0

    lax.fori_loop(0, steps + 3 - groups, turn, 0)

    cot_copy.wait()
    for h in range(HEADS_KV):
        cols = slice(h * HEAD_DIM, (h + 1) * HEAD_DIM)
        key = acc[0:tokens, cols]
        inv_scale = 1.0 / jnp.sqrt(
            jnp.sum(key * key, axis=1, keepdims=True) / HEAD_DIM + 1e-05
        )
        unit_key = key * inv_scale
        weighted = cot_ref[:, cols].astype(F32) * key_gain_ref[...]
        inner = jnp.sum(unit_key * weighted, axis=1, keepdims=True)
        back[0:tokens, cols] = (
            (weighted - unit_key * (inner / HEAD_DIM)) * inv_scale
        ).astype(jnp.bfloat16)
        inv_square = inv_scale * inv_scale

        def one_direction(j, _):
            at = pl.ds(pl.multiple_of(j * tokens, 128), tokens)
            tangent = acc[at, cols]
            shift = jnp.sum(unit_key * tangent, axis=1, keepdims=True) / HEAD_DIM
            across = jnp.sum(weighted * tangent, axis=1, keepdims=True)
            by_tangent = -inner * inv_square / HEAD_DIM
            by_key = (3.0 * shift * inner - across) * inv_square / HEAD_DIM
            by_weight = -shift * inv_square
            back[at, cols] = (
                tangent * by_tangent + unit_key * by_key + weighted * by_weight
            ).astype(jnp.bfloat16)
            return 0

        lax.fori_loop(1, count, one_direction, 0, unroll=True)

    def terms_of(owner):
        def one_pair(pair, _):
            cg = owner * 2 * groups + 2 * pair
            weight = jnp.concatenate([weight_at(cg), weight_at(cg + 1)], axis=0)
            normed = normed_at(owner * rows + pair * 2 * rows_g, 2 * rows_g)
            product = lax.dot_general(
                back[...], weight, (((1,), (1,)), ((), ())), preferred_element_type=F32
            )
            cols = pl.ds(pl.multiple_of(pair * 2 * rows_g, 128), 2 * rows_g)
            for j in range(count):
                part[owner, j : j + 1, cols] = jnp.sum(
                    product[j * tokens : (j + 1) * tokens] * normed, axis=0, keepdims=True
                )
            return 0

        lax.fori_loop(0, groups, one_pair, 0)

    def part_copy(b):
        owner = lax.rem(me + 1 + b, n)
        return pltpu.make_async_remote_copy(
            src_ref=part.at[owner],
            dst_ref=rbuf.at[me],
            send_sem=part_send.at[owner],
            recv_sem=part_recv.at[me],
            device_id=(dp, owner),
            device_id_type=MESH,
        )

    def send_part(b, _):
        terms_of(lax.rem(me + 1 + b, n))
        part_copy(b).start()
        return 0

    lax.fori_loop(0, n - 1, send_part, 0)
    terms_of(me)

    def take_part(b, run):
        other = lax.rem(me + n - 1 - b, n)
        pltpu.make_async_remote_copy(
            src_ref=part.at[other],
            dst_ref=rbuf.at[other],
            send_sem=part_send.at[other],
            recv_sem=part_recv.at[other],
            device_id=(dp, other),
            device_id_type=MESH,
        ).wait_recv()
        return run + rbuf[other]

    xbuf[dp] = lax.fori_loop(0, n - 1, take_part, part[me])

    def dp_copy(b, slot):
        other = lax.rem(dp + 1 + b, n_dp)
        return pltpu.make_async_remote_copy(
            src_ref=xbuf.at[dp if slot else other],
            dst_ref=xbuf.at[dp if slot else other],
            send_sem=dp_send.at[b],
            recv_sem=dp_recv.at[dp if slot else other],
            device_id=(other, me),
            device_id_type=MESH,
        )

    for b in range(n_dp - 1):
        dp_copy(b, True).start()
    for b in range(n_dp - 1):
        dp_copy(b, False).wait_recv()
    summed = xbuf[0]
    for d in range(1, n_dp):
        summed = summed + xbuf[d]
    summed = summed / math.sqrt(total_tokens)
    grad_ref[...] = summed[0:1]
    images = summed[1:count]
    dirs = count - 1
    lane = lax.broadcasted_iota(jnp.int32, (dirs, 128), 1)
    gram = jnp.zeros((dirs, 128), F32)
    for j in range(dirs):
        gram = jnp.where(
            lane == j, jnp.sum(images * images[j : j + 1], axis=1, keepdims=True), gram
        )
    gbuf[me] = gram

    def gram_copy(b, slot):
        other = lax.rem(me + 1 + b, n)
        return pltpu.make_async_remote_copy(
            src_ref=gbuf.at[me if slot else other],
            dst_ref=gbuf.at[me if slot else other],
            send_sem=gram_send.at[b],
            recv_sem=gram_recv.at[me if slot else other],
            device_id=(dp, other),
            device_id_type=MESH,
        )

    def start_gram(b, _):
        gram_copy(b, True).start()
        return 0

    def take_gram(b, _):
        gram_copy(b, False).wait_recv()
        return 0

    lax.fori_loop(0, n - 1, start_gram, 0)
    lax.fori_loop(0, n - 1, take_gram, 0)
    gram = lax.fori_loop(1, n, lambda s, run: run + gbuf[s], gbuf[0])

    row = lax.broadcasted_iota(jnp.int32, (dirs, 1), 0)
    for j in range(dirs):
        inverse = 1.0 / jnp.sqrt(gram[j : j + 1, j : j + 1])
        gram_row = gram[j : j + 1] * inverse
        image_row = images[j : j + 1] * inverse
        factor = jnp.where(row > j, gram[:, j : j + 1] * inverse, 0.0)
        gram = jnp.where(row == j, gram_row, gram - factor * gram_row)
        images = jnp.where(row == j, image_row, images - factor * image_row)
    ortho_ref[...] = math.sqrt(D) * images

    for g in range(groups):

        @pl.when(z + 1 < line)
        def _():
            sent(Z, g, True)

        @pl.when(z >= 1)
        def _():
            sent(ZB, g, True)

        for kind in (X, Y2, DX, DY2):
            sent(kind, g, True)

    def drain(i, _):
        @pl.when(passes_on(i))
        def _():
            sent(Z, i)

        for kind in (X, Y1, DZ, DY1, Y2, DX, DY2):
            sent(kind, i)
        return 0

    lax.fori_loop(groups, steps, drain, 0)

    def drain_parts(b, _):
        part_copy(b).wait_send()
        gram_copy(b, True).wait_send()
        return 0

    lax.fori_loop(0, n - 1, drain_parts, 0)
    for b in range(n_dp - 1):
        dp_copy(b, True).wait_send()


def per_device(n, n_dp, activations, gain, key_weight, key_gain, cotangent, directions):
    tokens, width = activations.shape
    rows, width_keys = key_weight.shape
    count = directions.shape[1] + 1
    groups = 2 if rows >= 1024 else 1
    rows_g = rows // (2 * groups)
    steps = n // 2 * groups
    factors = jnp.concatenate(
        [gain[None], directions.T, jnp.zeros((PAD - count, rows), jnp.bfloat16)], axis=0
    )
    factors = factors.reshape(PAD, 2 * groups, rows_g).transpose(1, 0, 2)
    factors = jnp.pad(factors, ((0, 0), (0, 0), (0, width_keys - rows_g)))
    vmem = pl.BlockSpec(memory_space=pltpu.VMEM)
    hbm = pl.BlockSpec(memory_space=pl.ANY)
    dma = pltpu.SemaphoreType.DMA
    flops = 4 * count * tokens * width * width_keys
    ortho, grad = pl.pallas_call(
        functools.partial(kernel, n, n_dp, groups, tokens * n * n_dp),
        out_shape=(
            jax.ShapeDtypeStruct((count - 1, rows), F32),
            jax.ShapeDtypeStruct((1, rows), F32),
        ),
        in_specs=[hbm, hbm, hbm, vmem, hbm],
        out_specs=(vmem, vmem),
        scratch_shapes=[
            pltpu.VMEM((tokens, width), jnp.bfloat16),
            pltpu.VMEM((tokens, width_keys), jnp.bfloat16),
            pltpu.VMEM((n * 2 * groups, rows_g + PAD, width_keys), jnp.bfloat16),
            pltpu.VMEM((count * tokens, 2 * rows_g), jnp.bfloat16),
            pltpu.VMEM((count * tokens, width_keys), F32),
            pltpu.VMEM((count * tokens, width_keys), jnp.bfloat16),
            pltpu.VMEM((n, count, rows), F32),
            pltpu.VMEM((n, count, rows), F32),
            pltpu.VMEM((n_dp, count, rows), F32),
            pltpu.VMEM((n, count - 1, 128), F32),
            pltpu.VMEM((tokens, width), F32),
            dma((3, 2 * groups)),
            dma((2,)),
            dma((9, steps)),
            dma((8, steps)),
            dma((n,)),
            dma((n,)),
            dma((n_dp,)),
            dma((n_dp,)),
            dma((n,)),
            dma((n,)),
        ],
        compiler_params=pltpu.CompilerParams(
            collective_id=0, has_side_effects=True, vmem_limit_bytes=56 * 1024 * 1024
        ),
        cost_estimate=pl.CostEstimate(flops=flops, bytes_accessed=4 * 2**20, transcendentals=0),
    )(activations, key_weight, factors, key_gain[None], cotangent)
    return (ortho.T, grad[0])


def solution(mesh):
    placed = (
        P(("dp", "fsdp"), None),
        P("fsdp"),
        P("fsdp", None),
        P(),
        P(("dp", "fsdp"), None),
        P("fsdp", None),
    )
    return jax.shard_map(
        functools.partial(per_device, mesh.shape["fsdp"], mesh.shape["dp"]),
        mesh=mesh,
        in_specs=placed,
        out_specs=(P("fsdp", None), P("fsdp")),
        check_vma=False,
    )
```

```python
import functools
import math

import jax
import jax.numpy as jnp
from jax import lax
from jax.experimental import pallas as pl
from jax.experimental.pallas import tpu as pltpu
from jax.sharding import PartitionSpec as P

D = 8192
HEADS_KV = 4
HEAD_DIM = 128
PAD = 16
MESH = pl.DeviceIdType.MESH
Z, Y1, DZ, DY1, X, Y2, DX, DY2 = range(8)
ZB = 8
F32 = jnp.float32


def kernel(
    n, n_dp, groups, total_tokens,
    act_in, w_ref, dg_ref, key_gain_ref, cot_in,
    ortho_ref, grad_ref,
    act_ref, cot_ref, wbuf, lifted, acc, back, part, rbuf, xbuf, gbuf, nbuf, own_sem, in_sem,
    send_sem, recv_sem, part_send, part_recv, dp_send, dp_recv, gram_send, gram_recv,
):
    line = n // 2
    steps = line * groups
    tokens = act_ref.shape[0]
    rows = w_ref.shape[0]
    rows_g = rows // (2 * groups)
    unit = rows_g // 4
    count = back.shape[0] // tokens
    dp, me = lax.axis_index("dp"), lax.axis_index("fsdp")
    core, y = lax.rem(dp, 2), dp // 2
    z, x = me // 2, lax.rem(me, 2)
    sibling = dp + 1 - 2 * core
    y_peer = lax.rem(dp + 2, n_dp)
    x_peer = me + 1 - 2 * x

    barrier = pltpu.get_barrier_semaphore()

    def greet_fsdp(b, _):
        pl.semaphore_signal(
            barrier, inc=1, device_id=(dp, lax.rem(me + 1 + b, n)), device_id_type=MESH
        )
        return 0

    def greet_dp(b, _):
        pl.semaphore_signal(
            barrier, inc=1, device_id=(lax.rem(dp + 1 + b, n_dp), me), device_id_type=MESH
        )
        return 0

    lax.fori_loop(0, n - 1, greet_fsdp, 0)
    lax.fori_loop(0, n_dp - 1, greet_dp, 0)

    def place(zp, xp, cp, g):
        return ((zp * 2 + xp) * 2 + cp) * groups + g

    own_copies = []
    for cg in range(2 * groups):
        at = me * 2 * groups + cg
        top, low = cg * rows_g, cg * rows_g + 2 * unit
        own_copies += [
            pltpu.make_async_copy(
                w_ref.at[top : top + 2 * unit], wbuf.at[at, 0 : 2 * unit], own_sem.at[0, cg]
            ),
            pltpu.make_async_copy(
                w_ref.at[low : low + 2 * unit],
                wbuf.at[at, 2 * unit + PAD : 4 * unit + PAD],
                own_sem.at[1, cg],
            ),
            pltpu.make_async_copy(
                dg_ref.at[cg], wbuf.at[at, 2 * unit : 2 * unit + PAD], own_sem.at[2, cg]
            ),
        ]
    for one in own_copies:
        one.start()
    act_copy = pltpu.make_async_copy(act_in, act_ref, in_sem.at[0])
    cot_copy = pltpu.make_async_copy(cot_in, cot_ref, in_sem.at[1])
    act_copy.start()
    cot_copy.start()

    room = jnp.minimum(z, line - 1 - z)
    wide = jnp.where(z < line - 1 - z, 1, -1)

    def source(k):
        near = k <= 2 * room
        dist = jnp.where(near, (k + 1) // 2, k - room)
        sign = jnp.where(near, jnp.where(lax.rem(k, 2) == 1, -1, 1), wide)
        return z + sign * dist, sign

    def span(kind, first, sent):
        side = y if sent else 1 - y
        if kind in (Z, ZB, DZ) or (first and kind in (X, DX)):
            start, size = y * unit, 3 * unit + PAD
        elif kind in (X, DX):
            start, size = y * (2 * unit), 2 * unit + PAD
        else:
            if kind in (DY1, DY2):
                side = 1 - y if sent else y
                side = 1 - y
            if kind in (Y1, DY1) or first:
                start, size = side * (3 * unit + PAD), unit
            else:
                start, size = side * (2 * unit + PAD), 2 * unit
        return pl.ds(pl.multiple_of(start, 16), size)

    def copy(kind, i, first, sent):
        k, g = i // groups, lax.rem(i, groups)
        zp, sign = source(k)
        own_column = kind in (Z, ZB, Y1, DZ, DY1)
        to_sibling = kind in (DZ, DY1, DX, DY2)
        if kind == X and sent:
            own_column = True
        column = x if own_column else 1 - x
        half = (core if sent else 1 - core) if to_sibling else core
        if kind == ZB:
            device = (dp, me - 2)
        elif kind == Z:
            device = (dp, me + 2) if first else (dp, me - 2 * sign)
        elif kind == X:
            device = (dp, x_peer)
        elif kind in (Y1, Y2):
            device = (y_peer, me)
        else:
            device = (sibling, me)
        ref = wbuf.at[place(zp, column, half, g), span(kind, first, sent)]
        arrival = Z if kind == ZB else kind
        return pltpu.make_async_remote_copy(
            src_ref=ref,
            dst_ref=ref,
            send_sem=send_sem.at[kind, i],
            recv_sem=recv_sem.at[arrival, zp * groups + g],
            device_id=device,
            device_id_type=MESH,
        )

    def start(kind, i, first=False):
        copy(kind, i, first, True).start()

    def arrive(kind, i, first=False):
        copy(kind, i, first, False).wait_recv()

    def sent(kind, i, first=False):
        copy(kind, i, first, True).wait_send()

    def passes_on(i):
        sign = source(i // groups)[1]
        onward = z - sign
        return (onward >= 0) & (onward < line)

    pl.semaphore_wait(barrier, n - 1 + n_dp - 1)
    for one in own_copies:
        one.wait()

    for g in range(groups):

        @pl.when(z + 1 < line)
        def _():
            start(Z, g, True)

        @pl.when(z >= 1)
        def _():
            start(ZB, g, True)

        start(X, g, True)

    act_copy.wait()

    width = act_ref.shape[1]

    def square_sum(q, run):
        part_in = act_ref[:, pl.ds(pl.multiple_of(q * 512, 512), 512)].astype(F32)
        part_in = part_in * part_in
        for h in range(4):
            run = run + part_in[:, h * 128 : (h + 1) * 128]
        return run

    square = lax.fori_loop(0, width // 512, square_sum, jnp.zeros((tokens, 128), F32))
    square = jnp.sum(square, axis=1, keepdims=True)
    rstd = jnp.broadcast_to(1.0 / jnp.sqrt(square / width + 1e-05), (tokens, 512))

    def normalize(q, _):
        cols = pl.ds(pl.multiple_of(q * 512, 512), 512)
        normed = act_ref[:, cols].astype(F32) * rstd
        nbuf[:, cols] = normed
        act_ref[:, cols] = normed.astype(jnp.bfloat16)
        return 0

    lax.fori_loop(0, width // 512, normalize, 0)

    def normed_at(feature, size):
        return nbuf[:, pl.ds(pl.multiple_of(feature, 128), size)]

    def weight_at(at):
        return jnp.concatenate(
            [wbuf[at, 0 : 2 * unit], wbuf[at, 2 * unit + PAD : 4 * unit + PAD]], axis=0
        )

    def forward(blocks, fresh=False):
        weights = []
        for b, (zp, xp, g) in enumerate(blocks):
            for cp in range(2):
                at = place(zp, xp, cp, g)
                feature = (zp * 2 + xp) * rows + (cp * groups + g) * rows_g
                normed = act_ref[:, pl.ds(pl.multiple_of(feature, 128), rows_g)]
                factors = wbuf[at, 2 * unit : 2 * unit + PAD, 0:rows_g].astype(F32)
                to = (2 * b + cp) * rows_g
                for j in range(count):
                    factor = jnp.broadcast_to(factors[j : j + 1], (16, rows_g))
                    factor = jnp.concatenate([factor.astype(jnp.bfloat16)] * (tokens // 16), axis=0)
                    lifted[j * tokens : (j + 1) * tokens, to : to + rows_g] = normed * factor
                weights.append(weight_at(at))
        weight = jnp.concatenate(weights, axis=0)
        for h in range(2):
            half = slice(h * 256, (h + 1) * 256)
            product = jnp.dot(
                lifted[:, 0 : len(weights) * rows_g], weight[:, half], preferred_element_type=F32
            )
            acc[:, half] = product if fresh else acc[:, half] + product

    forward([(z, x, g) for g in range(groups)], True)

    def cross_arrived(i, first):
        arrive(X, i, first)
        start(Y2, i, first)
        start(DX, i, first)

    def turn(t, _):
        i = t + groups

        @pl.when(i < steps)
        def _():
            arrive(Z, i)

            @pl.when(passes_on(i))
            def _():
                start(Z, i)

            start(X, i)
            start(Y1, i)
            start(DZ, i)

        if groups > 1:

            @pl.when(t == 0)
            def _():
                for early in range(groups - 1):
                    cross_arrived(early, True)

        i1 = t + groups - 1

        @pl.when(i1 < groups)
        def _():
            cross_arrived(i1, True)

        @pl.when((i1 >= groups) & (i1 < steps))
        def _():
            cross_arrived(i1, False)
            arrive(Y1, i1)
            start(DY1, i1)

        i2 = t + groups - 2

        @pl.when((i2 >= 0) & (i2 < groups))
        def _():
            arrive(Y2, i2, True)
            start(DY2, i2, True)

        @pl.when((i2 >= groups) & (i2 < steps))
        def _():
            arrive(Y2, i2)
            start(DY2, i2)
            arrive(DZ, i2)
            arrive(DY1, i2)

        i3 = t + groups - 3

        @pl.when((i3 >= 0) & (i3 < groups))
        def _():
            arrive(DX, i3, True)
            arrive(DY2, i3, True)

        @pl.when((i3 >= groups) & (i3 < steps))
        def _():
            arrive(DX, i3)
            arrive(DY2, i3)

        own = (source(i2 // groups)[0], x, lax.rem(i2, groups))
        cross = (source(i3 // groups)[0], 1 - x, lax.rem(i3, groups))
        both = (i2 >= groups) & (i2 < steps)

        @pl.when(both)
        def _():
            forward([own, cross])

        @pl.when((i3 >= 0) & (i3 < steps) & ((i2 < groups) | (i2 >= steps)))
        def _():
            forward([cross])

        return 0

    lax.fori_loop(0, steps + 3 - groups, turn, 0)

    cot_copy.wait()
    for h in range(HEADS_KV):
        cols = slice(h * HEAD_DIM, (h + 1) * HEAD_DIM)
        key = acc[0:tokens, cols]
        inv_scale = 1.0 / jnp.sqrt(
            jnp.sum(key * key, axis=1, keepdims=True) / HEAD_DIM + 1e-05
        )
        unit_key = key * inv_scale
        weighted = cot_ref[:, cols].astype(F32) * key_gain_ref[...]
        inner = jnp.sum(unit_key * weighted, axis=1, keepdims=True)
        back[0:tokens, cols] = (
            (weighted - unit_key * (inner / HEAD_DIM)) * inv_scale
        ).astype(jnp.bfloat16)
        inv_square = inv_scale * inv_scale

        def one_direction(j, _):
            at = pl.ds(pl.multiple_of(j * tokens, 128), tokens)
            tangent = acc[at, cols]
            shift = jnp.sum(unit_key * tangent, axis=1, keepdims=True) / HEAD_DIM
            across = jnp.sum(weighted * tangent, axis=1, keepdims=True)
            by_tangent = -inner * inv_square / HEAD_DIM
            by_key = (3.0 * shift * inner - across) * inv_square / HEAD_DIM
            by_weight = -shift * inv_square
            back[at, cols] = (
                tangent * by_tangent + unit_key * by_key + weighted * by_weight
            ).astype(jnp.bfloat16)
            return 0

        lax.fori_loop(1, count, one_direction, 0, unroll=True)

    def terms_of(owner):
        def one_pair(pair, _):
            cg = owner * 2 * groups + 2 * pair
            weight = jnp.concatenate([weight_at(cg), weight_at(cg + 1)], axis=0)
            normed = normed_at(owner * rows + pair * 2 * rows_g, 2 * rows_g)
            product = lax.dot_general(
                back[...], weight, (((1,), (1,)), ((), ())), preferred_element_type=F32
            )
            cols = pl.ds(pl.multiple_of(pair * 2 * rows_g, 128), 2 * rows_g)
            for j in range(count):
                part[owner, j : j + 1, cols] = jnp.sum(
                    product[j * tokens : (j + 1) * tokens] * normed, axis=0, keepdims=True
                )
            return 0

        lax.fori_loop(0, groups, one_pair, 0)

    def part_copy(b):
        owner = lax.rem(me + 1 + b, n)
        return pltpu.make_async_remote_copy(
            src_ref=part.at[owner],
            dst_ref=rbuf.at[me],
            send_sem=part_send.at[owner],
            recv_sem=part_recv.at[me],
            device_id=(dp, owner),
            device_id_type=MESH,
        )

    def send_part(b, _):
        terms_of(lax.rem(me + 1 + b, n))
        part_copy(b).start()
        return 0

    lax.fori_loop(0, n - 1, send_part, 0)
    terms_of(me)

    def take_part(b, run):
        other = lax.rem(me + n - 1 - b, n)
        pltpu.make_async_remote_copy(
            src_ref=part.at[other],
            dst_ref=rbuf.at[other],
            send_sem=part_send.at[other],
            recv_sem=part_recv.at[other],
            device_id=(dp, other),
            device_id_type=MESH,
        ).wait_recv()
        return run + rbuf[other]

    xbuf[dp] = lax.fori_loop(0, n - 1, take_part, part[me])

    def dp_copy(b, slot):
        other = lax.rem(dp + 1 + b, n_dp)
        return pltpu.make_async_remote_copy(
            src_ref=xbuf.at[dp if slot else other],
            dst_ref=xbuf.at[dp if slot else other],
            send_sem=dp_send.at[b],
            recv_sem=dp_recv.at[dp if slot else other],
            device_id=(other, me),
            device_id_type=MESH,
        )

    for b in range(n_dp - 1):
        dp_copy(b, True).start()
    for b in range(n_dp - 1):
        dp_copy(b, False).wait_recv()
    summed = xbuf[0]
    for d in range(1, n_dp):
        summed = summed + xbuf[d]
    summed = summed / math.sqrt(total_tokens)
    grad_ref[...] = summed[0:1]
    images = summed[1:count]
    dirs = count - 1
    lane = lax.broadcasted_iota(jnp.int32, (dirs, 128), 1)
    gram = jnp.zeros((dirs, 128), F32)
    for j in range(dirs):
        gram = jnp.where(
            lane == j, jnp.sum(images * images[j : j + 1], axis=1, keepdims=True), gram
        )
    gbuf[me] = gram

    def gram_copy(b, slot):
        other = lax.rem(me + 1 + b, n)
        return pltpu.make_async_remote_copy(
            src_ref=gbuf.at[me if slot else other],
            dst_ref=gbuf.at[me if slot else other],
            send_sem=gram_send.at[b],
            recv_sem=gram_recv.at[me if slot else other],
            device_id=(dp, other),
            device_id_type=MESH,
        )

    def start_gram(b, _):
        gram_copy(b, True).start()
        return 0

    def take_gram(b, _):
        gram_copy(b, False).wait_recv()
        return 0

    lax.fori_loop(0, n - 1, start_gram, 0)
    lax.fori_loop(0, n - 1, take_gram, 0)
    gram = lax.fori_loop(1, n, lambda s, run: run + gbuf[s], gbuf[0])

    row = lax.broadcasted_iota(jnp.int32, (dirs, 1), 0)
    for j in range(dirs):
        inverse = 1.0 / jnp.sqrt(gram[j : j + 1, j : j + 1])
        gram_row = gram[j : j + 1] * inverse
        image_row = images[j : j + 1] * inverse
        factor = jnp.where(row > j, gram[:, j : j + 1] * inverse, 0.0)
        gram = jnp.where(row == j, gram_row, gram - factor * gram_row)
        images = jnp.where(row == j, image_row, images - factor * image_row)
    ortho_ref[...] = math.sqrt(D) * images

    for g in range(groups):

        @pl.when(z + 1 < line)
        def _():
            sent(Z, g, True)

        @pl.when(z >= 1)
        def _():
            sent(ZB, g, True)

        for kind in (X, Y2, DX, DY2):
            sent(kind, g, True)

    def drain(i, _):
        @pl.when(passes_on(i))
        def _():
            sent(Z, i)

        for kind in (X, Y1, DZ, DY1, Y2, DX, DY2):
            sent(kind, i)
        return 0

    lax.fori_loop(groups, steps, drain, 0)

    def drain_parts(b, _):
        part_copy(b).wait_send()
        gram_copy(b, True).wait_send()
        return 0

    lax.fori_loop(0, n - 1, drain_parts, 0)
    for b in range(n_dp - 1):
        dp_copy(b, True).wait_send()


def per_device(n, n_dp, activations, gain, key_weight, key_gain, cotangent, directions):
    tokens, width = activations.shape
    rows, width_keys = key_weight.shape
    count = directions.shape[1] + 1
    groups = 2 if rows >= 1024 else 1
    rows_g = rows // (2 * groups)
    steps = n // 2 * groups
    factors = jnp.concatenate(
        [gain[None], directions.T, jnp.zeros((PAD - count, rows), jnp.bfloat16)], axis=0
    )
    factors = factors.reshape(PAD, 2 * groups, rows_g).transpose(1, 0, 2)
    factors = jnp.pad(factors, ((0, 0), (0, 0), (0, width_keys - rows_g)))
    vmem = pl.BlockSpec(memory_space=pltpu.VMEM)
    hbm = pl.BlockSpec(memory_space=pl.ANY)
    dma = pltpu.SemaphoreType.DMA
    flops = 4 * count * tokens * width * width_keys
    ortho, grad = pl.pallas_call(
        functools.partial(kernel, n, n_dp, groups, tokens * n * n_dp),
        out_shape=(
            jax.ShapeDtypeStruct((count - 1, rows), F32),
            jax.ShapeDtypeStruct((1, rows), F32),
        ),
        in_specs=[hbm, hbm, hbm, vmem, hbm],
        out_specs=(vmem, vmem),
        scratch_shapes=[
            pltpu.VMEM((tokens, width), jnp.bfloat16),
            pltpu.VMEM((tokens, width_keys), jnp.bfloat16),
            pltpu.VMEM((n * 2 * groups, rows_g + PAD, width_keys), jnp.bfloat16),
            pltpu.VMEM((count * tokens, 4 * rows_g), jnp.bfloat16),
            pltpu.VMEM((count * tokens, width_keys), F32),
            pltpu.VMEM((count * tokens, width_keys), jnp.bfloat16),
            pltpu.VMEM((n, count, rows), F32),
            pltpu.VMEM((n, count, rows), F32),
            pltpu.VMEM((n_dp, count, rows), F32),
            pltpu.VMEM((n, count - 1, 128), F32),
            pltpu.VMEM((tokens, width), F32),
            dma((3, 2 * groups)),
            dma((2,)),
            dma((9, steps)),
            dma((8, steps)),
            dma((n,)),
            dma((n,)),
            dma((n_dp,)),
            dma((n_dp,)),
            dma((n,)),
            dma((n,)),
        ],
        compiler_params=pltpu.CompilerParams(
            collective_id=0, has_side_effects=True, vmem_limit_bytes=56 * 1024 * 1024
        ),
        cost_estimate=pl.CostEstimate(flops=flops, bytes_accessed=4 * 2**20, transcendentals=0),
    )(activations, key_weight, factors, key_gain[None], cotangent)
    return (ortho.T, grad[0])


def solution(mesh):
    placed = (
        P(("dp", "fsdp"), None),
        P("fsdp"),
        P("fsdp", None),
        P(),
        P(("dp", "fsdp"), None),
        P("fsdp", None),
    )
    return jax.shard_map(
        functools.partial(per_device, mesh.shape["fsdp"], mesh.shape["dp"]),
        mesh=mesh,
        in_specs=placed,
        out_specs=(P("fsdp", None), P("fsdp")),
        check_vma=False,
    )
```

```python
import functools
import math

import jax
import jax.numpy as jnp
from jax import lax
from jax.experimental import pallas as pl
from jax.experimental.pallas import tpu as pltpu
from jax.sharding import PartitionSpec as P

D = 8192
HEADS_KV = 4
HEAD_DIM = 128
PAD = 16
MESH = pl.DeviceIdType.MESH
Z, Y1, DZ, DY1, X, Y2, DX, DY2 = range(8)
ZB = 8
F32 = jnp.float32


def kernel(
    n, n_dp, groups, total_tokens,
    act_in, w_ref, dg_ref, key_gain_ref, cot_in,
    ortho_ref, grad_ref,
    act_ref, cot_ref, wbuf, turned, lifted, acc, back, part, rbuf, xbuf, gbuf, nbuf, own_sem, in_sem,
    send_sem, recv_sem, part_send, part_recv, dp_send, dp_recv, gram_send, gram_recv,
):
    line = n // 2
    steps = line * groups
    tokens = act_ref.shape[0]
    rows = w_ref.shape[0]
    rows_g = rows // (2 * groups)
    unit = rows_g // 4
    count = back.shape[0] // tokens
    dp, me = lax.axis_index("dp"), lax.axis_index("fsdp")
    core, y = lax.rem(dp, 2), dp // 2
    z, x = me // 2, lax.rem(me, 2)
    sibling = dp + 1 - 2 * core
    y_peer = lax.rem(dp + 2, n_dp)
    x_peer = me + 1 - 2 * x

    barrier = pltpu.get_barrier_semaphore()

    def greet_fsdp(b, _):
        pl.semaphore_signal(
            barrier, inc=1, device_id=(dp, lax.rem(me + 1 + b, n)), device_id_type=MESH
        )
        return 0

    def greet_dp(b, _):
        pl.semaphore_signal(
            barrier, inc=1, device_id=(lax.rem(dp + 1 + b, n_dp), me), device_id_type=MESH
        )
        return 0

    lax.fori_loop(0, n - 1, greet_fsdp, 0)
    lax.fori_loop(0, n_dp - 1, greet_dp, 0)

    def place(zp, xp, cp, g):
        return ((zp * 2 + xp) * 2 + cp) * groups + g

    own_copies = []
    for cg in range(2 * groups):
        at = me * 2 * groups + cg
        top, low = cg * rows_g, cg * rows_g + 2 * unit
        own_copies += [
            pltpu.make_async_copy(
                w_ref.at[top : top + 2 * unit], wbuf.at[at, 0 : 2 * unit], own_sem.at[0, cg]
            ),
            pltpu.make_async_copy(
                w_ref.at[low : low + 2 * unit],
                wbuf.at[at, 2 * unit + PAD : 4 * unit + PAD],
                own_sem.at[1, cg],
            ),
            pltpu.make_async_copy(
                dg_ref.at[cg], wbuf.at[at, 2 * unit : 2 * unit + PAD], own_sem.at[2, cg]
            ),
        ]
    for one in own_copies:
        one.start()
    act_copy = pltpu.make_async_copy(act_in, act_ref, in_sem.at[0])
    cot_copy = pltpu.make_async_copy(cot_in, cot_ref, in_sem.at[1])
    act_copy.start()
    cot_copy.start()

    room = jnp.minimum(z, line - 1 - z)
    wide = jnp.where(z < line - 1 - z, 1, -1)

    def source(k):
        near = k <= 2 * room
        dist = jnp.where(near, (k + 1) // 2, k - room)
        sign = jnp.where(near, jnp.where(lax.rem(k, 2) == 1, -1, 1), wide)
        return z + sign * dist, sign

    def span(kind, first, sent):
        side = y if sent else 1 - y
        if kind in (Z, ZB, DZ) or (first and kind in (X, DX)):
            start, size = y * unit, 3 * unit + PAD
        elif kind in (X, DX):
            start, size = y * (2 * unit), 2 * unit + PAD
        else:
            if kind in (DY1, DY2):
                side = 1 - y if sent else y
                side = 1 - y
            if kind in (Y1, DY1) or first:
                start, size = side * (3 * unit + PAD), unit
            else:
                start, size = side * (2 * unit + PAD), 2 * unit
        return pl.ds(pl.multiple_of(start, 16), size)

    def copy(kind, i, first, sent):
        k, g = i // groups, lax.rem(i, groups)
        zp, sign = source(k)
        own_column = kind in (Z, ZB, Y1, DZ, DY1)
        to_sibling = kind in (DZ, DY1, DX, DY2)
        if kind == X and sent:
            own_column = True
        column = x if own_column else 1 - x
        half = (core if sent else 1 - core) if to_sibling else core
        if kind == ZB:
            device = (dp, me - 2)
        elif kind == Z:
            device = (dp, me + 2) if first else (dp, me - 2 * sign)
        elif kind == X:
            device = (dp, x_peer)
        elif kind in (Y1, Y2):
            device = (y_peer, me)
        else:
            device = (sibling, me)
        ref = wbuf.at[place(zp, column, half, g), span(kind, first, sent)]
        arrival = Z if kind == ZB else kind
        return pltpu.make_async_remote_copy(
            src_ref=ref,
            dst_ref=ref,
            send_sem=send_sem.at[kind, i],
            recv_sem=recv_sem.at[arrival, zp * groups + g],
            device_id=device,
            device_id_type=MESH,
        )

    def start(kind, i, first=False):
        copy(kind, i, first, True).start()

    def arrive(kind, i, first=False):
        copy(kind, i, first, False).wait_recv()

    def sent(kind, i, first=False):
        copy(kind, i, first, True).wait_send()

    def passes_on(i):
        sign = source(i // groups)[1]
        onward = z - sign
        return (onward >= 0) & (onward < line)

    pl.semaphore_wait(barrier, n - 1 + n_dp - 1)
    for one in own_copies:
        one.wait()

    for g in range(groups):

        @pl.when(z + 1 < line)
        def _():
            start(Z, g, True)

        @pl.when(z >= 1)
        def _():
            start(ZB, g, True)

        start(X, g, True)

    act_copy.wait()

    width = act_ref.shape[1]

    def square_sum(q, run):
        part_in = act_ref[:, pl.ds(pl.multiple_of(q * 512, 512), 512)].astype(F32)
        part_in = part_in * part_in
        for h in range(4):
            run = run + part_in[:, h * 128 : (h + 1) * 128]
        return run

    square = lax.fori_loop(0, width // 512, square_sum, jnp.zeros((tokens, 128), F32))
    square = jnp.sum(square, axis=1, keepdims=True)
    rstd = jnp.broadcast_to(1.0 / jnp.sqrt(square / width + 1e-05), (tokens, 512))

    def normalize(q, _):
        cols = pl.ds(pl.multiple_of(q * 512, 512), 512)
        nbuf[:, cols] = act_ref[:, cols].astype(F32) * rstd
        return 0

    lax.fori_loop(0, width // 512, normalize, 0)

    def normed_at(feature, size):
        return nbuf[:, pl.ds(pl.multiple_of(feature, 128), size)]

    def weight_at(at):
        return jnp.concatenate(
            [wbuf[at, 0 : 2 * unit], wbuf[at, 2 * unit + PAD : 4 * unit + PAD]], axis=0
        )

    def forward(blocks, fresh=False):
        weights = []
        for b, (zp, xp, g) in enumerate(blocks):
            for cp in range(2):
                at = place(zp, xp, cp, g)
                feature = (zp * 2 + xp) * rows + (cp * groups + g) * rows_g
                normed = normed_at(feature, rows_g)
                factors = wbuf[at, 2 * unit : 2 * unit + PAD, 0:rows_g].astype(F32)
                to = (2 * b + cp) * rows_g
                for j in range(count):
                    lifted[j * tokens : (j + 1) * tokens, to : to + rows_g] = (
                        normed * factors[j : j + 1]
                    ).astype(jnp.bfloat16)
                weights.append(weight_at(at))
                turned[:, pl.ds(pl.multiple_of(feature, 128), rows_g)] = weights[-1].T
        weight = jnp.concatenate(weights, axis=0)
        for h in range(2):
            half = slice(h * 256, (h + 1) * 256)
            product = jnp.dot(
                lifted[:, 0 : len(weights) * rows_g], weight[:, half], preferred_element_type=F32
            )
            acc[:, half] = product if fresh else acc[:, half] + product

    forward([(z, x, g) for g in range(groups)], True)

    def cross_arrived(i, first):
        arrive(X, i, first)
        start(Y2, i, first)
        start(DX, i, first)

    def turn(t, _):
        i = t + groups

        @pl.when(i < steps)
        def _():
            arrive(Z, i)

            @pl.when(passes_on(i))
            def _():
                start(Z, i)

            start(X, i)
            start(Y1, i)
            start(DZ, i)

        if groups > 1:

            @pl.when(t == 0)
            def _():
                for early in range(groups - 1):
                    cross_arrived(early, True)

        i1 = t + groups - 1

        @pl.when(i1 < groups)
        def _():
            cross_arrived(i1, True)

        @pl.when((i1 >= groups) & (i1 < steps))
        def _():
            cross_arrived(i1, False)
            arrive(Y1, i1)
            start(DY1, i1)

        i2 = t + groups - 2

        @pl.when((i2 >= 0) & (i2 < groups))
        def _():
            arrive(Y2, i2, True)
            start(DY2, i2, True)

        @pl.when((i2 >= groups) & (i2 < steps))
        def _():
            arrive(Y2, i2)
            start(DY2, i2)
            arrive(DZ, i2)
            arrive(DY1, i2)

        i3 = t + groups - 3

        @pl.when((i3 >= 0) & (i3 < groups))
        def _():
            arrive(DX, i3, True)
            arrive(DY2, i3, True)

        @pl.when((i3 >= groups) & (i3 < steps))
        def _():
            arrive(DX, i3)
            arrive(DY2, i3)

        own = (source(i2 // groups)[0], x, lax.rem(i2, groups))
        cross = (source(i3 // groups)[0], 1 - x, lax.rem(i3, groups))
        both = (i2 >= groups) & (i2 < steps)

        @pl.when(both)
        def _():
            forward([own, cross])

        @pl.when((i3 >= 0) & (i3 < steps) & ((i2 < groups) | (i2 >= steps)))
        def _():
            forward([cross])

        return 0

    lax.fori_loop(0, steps + 3 - groups, turn, 0)

    cot_copy.wait()
    for h in range(HEADS_KV):
        cols = slice(h * HEAD_DIM, (h + 1) * HEAD_DIM)
        key = acc[0:tokens, cols]
        inv_scale = 1.0 / jnp.sqrt(
            jnp.sum(key * key, axis=1, keepdims=True) / HEAD_DIM + 1e-05
        )
        unit_key = key * inv_scale
        weighted = cot_ref[:, cols].astype(F32) * key_gain_ref[...]
        inner = jnp.sum(unit_key * weighted, axis=1, keepdims=True)
        back[0:tokens, cols] = (
            (weighted - unit_key * (inner / HEAD_DIM)) * inv_scale
        ).astype(jnp.bfloat16)
        inv_square = inv_scale * inv_scale

        def one_direction(j, _):
            at = pl.ds(pl.multiple_of(j * tokens, 128), tokens)
            tangent = acc[at, cols]
            shift = jnp.sum(unit_key * tangent, axis=1, keepdims=True) / HEAD_DIM
            across = jnp.sum(weighted * tangent, axis=1, keepdims=True)
            by_tangent = -inner * inv_square / HEAD_DIM
            by_key = (3.0 * shift * inner - across) * inv_square / HEAD_DIM
            by_weight = -shift * inv_square
            back[at, cols] = (
                tangent * by_tangent + unit_key * by_key + weighted * by_weight
            ).astype(jnp.bfloat16)
            return 0

        lax.fori_loop(1, count, one_direction, 0, unroll=True)

    def terms_of(owner):
        def one_pair(pair, _):
            feature = owner * rows + pair * 2 * rows_g
            weight = turned[:, pl.ds(pl.multiple_of(feature, 128), 2 * rows_g)]
            normed = normed_at(feature, 2 * rows_g)
            product = jnp.dot(back[...], weight, preferred_element_type=F32)
            cols = pl.ds(pl.multiple_of(pair * 2 * rows_g, 128), 2 * rows_g)
            for j in range(count):
                part[owner, j : j + 1, cols] = jnp.sum(
                    product[j * tokens : (j + 1) * tokens] * normed, axis=0, keepdims=True
                )
            return 0

        lax.fori_loop(0, groups, one_pair, 0)

    def part_copy(b):
        owner = lax.rem(me + 1 + b, n)
        return pltpu.make_async_remote_copy(
            src_ref=part.at[owner],
            dst_ref=rbuf.at[me],
            send_sem=part_send.at[owner],
            recv_sem=part_recv.at[me],
            device_id=(dp, owner),
            device_id_type=MESH,
        )

    def send_part(b, _):
        terms_of(lax.rem(me + 1 + b, n))
        part_copy(b).start()
        return 0

    lax.fori_loop(0, n - 1, send_part, 0)
    terms_of(me)

    def take_part(b, run):
        other = lax.rem(me + n - 1 - b, n)
        pltpu.make_async_remote_copy(
            src_ref=part.at[other],
            dst_ref=rbuf.at[other],
            send_sem=part_send.at[other],
            recv_sem=part_recv.at[other],
            device_id=(dp, other),
            device_id_type=MESH,
        ).wait_recv()
        return run + rbuf[other]

    xbuf[dp] = lax.fori_loop(0, n - 1, take_part, part[me])

    def dp_copy(b, slot):
        other = lax.rem(dp + 1 + b, n_dp)
        return pltpu.make_async_remote_copy(
            src_ref=xbuf.at[dp if slot else other],
            dst_ref=xbuf.at[dp if slot else other],
            send_sem=dp_send.at[b],
            recv_sem=dp_recv.at[dp if slot else other],
            device_id=(other, me),
            device_id_type=MESH,
        )

    for b in range(n_dp - 1):
        dp_copy(b, True).start()
    for b in range(n_dp - 1):
        dp_copy(b, False).wait_recv()
    summed = xbuf[0]
    for d in range(1, n_dp):
        summed = summed + xbuf[d]
    summed = summed / math.sqrt(total_tokens)
    grad_ref[...] = summed[0:1]
    images = summed[1:count]
    dirs = count - 1
    lane = lax.broadcasted_iota(jnp.int32, (dirs, 128), 1)
    gram = jnp.zeros((dirs, 128), F32)
    for j in range(dirs):
        gram = jnp.where(
            lane == j, jnp.sum(images * images[j : j + 1], axis=1, keepdims=True), gram
        )
    gbuf[me] = gram

    def gram_copy(b, slot):
        other = lax.rem(me + 1 + b, n)
        return pltpu.make_async_remote_copy(
            src_ref=gbuf.at[me if slot else other],
            dst_ref=gbuf.at[me if slot else other],
            send_sem=gram_send.at[b],
            recv_sem=gram_recv.at[me if slot else other],
            device_id=(dp, other),
            device_id_type=MESH,
        )

    def start_gram(b, _):
        gram_copy(b, True).start()
        return 0

    def take_gram(b, _):
        gram_copy(b, False).wait_recv()
        return 0

    lax.fori_loop(0, n - 1, start_gram, 0)
    lax.fori_loop(0, n - 1, take_gram, 0)
    gram = lax.fori_loop(1, n, lambda s, run: run + gbuf[s], gbuf[0])

    row = lax.broadcasted_iota(jnp.int32, (dirs, 1), 0)
    for j in range(dirs):
        inverse = 1.0 / jnp.sqrt(gram[j : j + 1, j : j + 1])
        gram_row = gram[j : j + 1] * inverse
        image_row = images[j : j + 1] * inverse
        factor = jnp.where(row > j, gram[:, j : j + 1] * inverse, 0.0)
        gram = jnp.where(row == j, gram_row, gram - factor * gram_row)
        images = jnp.where(row == j, image_row, images - factor * image_row)
    ortho_ref[...] = math.sqrt(D) * images

    for g in range(groups):

        @pl.when(z + 1 < line)
        def _():
            sent(Z, g, True)

        @pl.when(z >= 1)
        def _():
            sent(ZB, g, True)

        for kind in (X, Y2, DX, DY2):
            sent(kind, g, True)

    def drain(i, _):
        @pl.when(passes_on(i))
        def _():
            sent(Z, i)

        for kind in (X, Y1, DZ, DY1, Y2, DX, DY2):
            sent(kind, i)
        return 0

    lax.fori_loop(groups, steps, drain, 0)

    def drain_parts(b, _):
        part_copy(b).wait_send()
        gram_copy(b, True).wait_send()
        return 0

    lax.fori_loop(0, n - 1, drain_parts, 0)
    for b in range(n_dp - 1):
        dp_copy(b, True).wait_send()


def per_device(n, n_dp, activations, gain, key_weight, key_gain, cotangent, directions):
    tokens, width = activations.shape
    rows, width_keys = key_weight.shape
    count = directions.shape[1] + 1
    groups = 2 if rows >= 1024 else 1
    rows_g = rows // (2 * groups)
    steps = n // 2 * groups
    factors = jnp.concatenate(
        [gain[None], directions.T, jnp.zeros((PAD - count, rows), jnp.bfloat16)], axis=0
    )
    factors = factors.reshape(PAD, 2 * groups, rows_g).transpose(1, 0, 2)
    factors = jnp.pad(factors, ((0, 0), (0, 0), (0, width_keys - rows_g)))
    vmem = pl.BlockSpec(memory_space=pltpu.VMEM)
    hbm = pl.BlockSpec(memory_space=pl.ANY)
    dma = pltpu.SemaphoreType.DMA
    flops = 4 * count * tokens * width * width_keys
    ortho, grad = pl.pallas_call(
        functools.partial(kernel, n, n_dp, groups, tokens * n * n_dp),
        out_shape=(
            jax.ShapeDtypeStruct((count - 1, rows), F32),
            jax.ShapeDtypeStruct((1, rows), F32),
        ),
        in_specs=[hbm, hbm, hbm, vmem, hbm],
        out_specs=(vmem, vmem),
        scratch_shapes=[
            pltpu.VMEM((tokens, width), jnp.bfloat16),
            pltpu.VMEM((tokens, width_keys), jnp.bfloat16),
            pltpu.VMEM((n * 2 * groups, rows_g + PAD, width_keys), jnp.bfloat16),
            pltpu.VMEM((width_keys, width), jnp.bfloat16),
            pltpu.VMEM((count * tokens, 4 * rows_g), jnp.bfloat16),
            pltpu.VMEM((count * tokens, width_keys), F32),
            pltpu.VMEM((count * tokens, width_keys), jnp.bfloat16),
            pltpu.VMEM((n, count, rows), F32),
            pltpu.VMEM((n, count, rows), F32),
            pltpu.VMEM((n_dp, count, rows), F32),
            pltpu.VMEM((n, count - 1, 128), F32),
            pltpu.VMEM((tokens, width), F32),
            dma((3, 2 * groups)),
            dma((2,)),
            dma((9, steps)),
            dma((8, steps)),
            dma((n,)),
            dma((n,)),
            dma((n_dp,)),
            dma((n_dp,)),
            dma((n,)),
            dma((n,)),
        ],
        compiler_params=pltpu.CompilerParams(
            collective_id=0, has_side_effects=True, vmem_limit_bytes=56 * 1024 * 1024
        ),
        cost_estimate=pl.CostEstimate(flops=flops, bytes_accessed=4 * 2**20, transcendentals=0),
    )(activations, key_weight, factors, key_gain[None], cotangent)
    return (ortho.T, grad[0])


def solution(mesh):
    placed = (
        P(("dp", "fsdp"), None),
        P("fsdp"),
        P("fsdp", None),
        P(),
        P(("dp", "fsdp"), None),
        P("fsdp", None),
    )
    return jax.shard_map(
        functools.partial(per_device, mesh.shape["fsdp"], mesh.shape["dp"]),
        mesh=mesh,
        in_specs=placed,
        out_specs=(P("fsdp", None), P("fsdp")),
        check_vma=False,
    )
```
